32 devices in a mesh: groups: 1, tok: 32 (over z, y, x, core).
Axes of the slice: x: 2, y: 2, z: 4, core: 2. Of those that a mesh axis runs over, the one named last changes fastest.
Arguments:
- clean_keys: bfloat16 [8192, 2048], P(('groups', 'tok')), may hold values from -12.5 to 12.5
- clean_values: bfloat16 [8192, 2048], P(('groups', 'tok')), may hold values from -12 to 12
- clean_rates: float32 [8192, 4], P(('groups', 'tok')), may hold values from 0.2 to 3.75
- w_in: bfloat16 [4, 512, 512], replicated, may hold values from -0.25 to 0.25
- w_gate: bfloat16 [4, 512, 512], replicated, may hold values from -0.25 to 0.25
- w_out: bfloat16 [4, 512, 512], replicated, may hold values from -0.25 to 0.25
- noisy_tokens: bfloat16 [8192, 2048], P(('groups', 'tok')), may hold values from -5 to 5
- swa_keys: bfloat16 [8192, 2048], P(('groups', 'tok')), may hold values from -250 to 250
- swa_values: bfloat16 [8192, 2048], P(('groups', 'tok')), may hold values from -30 to 30
- level_ids: int32 [64], P(('groups', 'tok')), may hold values from 0 to 7
- window_reach: int32 [64], P(('groups', 'tok')), may hold values from 2 to 1024, as said below
- level_mod: float32 [8, 4096], replicated, may hold values from -3 to 3
- mem_gain: float32 [2048], replicated, may hold values from 0.1 to 1.9
Outputs:
- layer_out: bfloat16 [8192, 2048], P(('groups', 'tok'))
The draws below stay inside these ranges and needn't reach their ends.
Inputs may be any that keep to these rules, and one draw needn't show every extreme that they name: `window_reach`: number of latest positions, the token's own included, that each block of noisy tokens attends to; some block has 1024.
All inputs are finite; a program needn't handle non-finite values.
Results may differ from the reference program's by a relative error of at most 0.0063.
The reference program's roundings to bfloat16 on the way count: a program that leaves them out, or rounds other values in their place, can miss the bound.
Values may be sent and summed in bfloat16 or wider, within the bound.
A program may use at most 128 MiB of HBM per device.

```python
import jax
import jax.numpy as jnp
from jax import lax

H = 4
DH = 512
D = 2048
SWDH = 128
WIN = 1024
BLOCK = 128
NLEVEL = 8
TOKENS = 8192
FRAMES = 64


def draw_clean_keys(key, part):
    scale_key = jax.random.fold_in(key, 61)
    noise_key = jax.random.fold_in(key, 67)
    feature_scale = jnp.exp(jax.random.uniform(scale_key, (D,), jnp.float32, -1.2, 1.1))
    noise = jnp.clip(jax.random.normal(noise_key, (TOKENS, D), jnp.float32), -4.0, 4.0)
    return (noise * feature_scale[None, :]).astype(jnp.bfloat16)


def draw_clean_values(key, part):
    scale_key = jax.random.fold_in(key, 71)
    noise_key = jax.random.fold_in(key, 73)
    pick_key = jax.random.fold_in(key, 79)
    sign_key = jax.random.fold_in(key, 83)
    feature_scale = jnp.exp(jax.random.uniform(scale_key, (D,), jnp.float32, -1.5, 1.0))
    picked = (jax.random.uniform(pick_key, (D,), jnp.float32) < 0.0625).astype(jnp.float32)
    sign = jnp.where(jax.random.uniform(sign_key, (D,), jnp.float32) < 0.5, -1.0, 1.0)
    noise = jnp.clip(jax.random.normal(noise_key, (TOKENS, D), jnp.float32), -4.0, 4.0)
    shared = 0.6
    return (noise * feature_scale[None, :] + (shared * sign * picked)[None, :]).astype(jnp.bfloat16)


def draw_clean_rates(key, part):
    head_key = jax.random.fold_in(key, 41)
    token_key = jax.random.fold_in(key, 43)
    ramp_up = 0.5 * 3.0 ** (jnp.arange(H, dtype=jnp.float32) / max(H - 1, 1))
    jitter = jax.random.uniform(head_key, (H,), jnp.float32, 0.8, 1.25)
    spread = jnp.exp(jax.random.uniform(token_key, (TOKENS, H), jnp.float32, jnp.log(0.5), jnp.log(2.0)))
    return (ramp_up * jitter)[None, :] * spread


def paired_features(key):
    base_key = jax.random.fold_in(key, 17)
    queries = jnp.clip(jax.random.normal(jax.random.fold_in(base_key, 1), (TOKENS, D), jnp.float32), -5.0, 5.0)
    key_draw = jnp.clip(jax.random.normal(jax.random.fold_in(base_key, 2), (TOKENS, D), jnp.float32), -5.0, 5.0)
    return (queries, key_draw)


def draw_noisy_tokens(key, part):
    return paired_features(key)[0].astype(jnp.bfloat16)


def draw_swa_keys(key, part):
    return paired_features(key)[1].astype(jnp.bfloat16)


def draw_window_reach(key, part):
    reach_key = jax.random.fold_in(key, 29)
    spot_key = jax.random.fold_in(key, 31)
    drawn = jax.random.randint(reach_key, (FRAMES,), 2, WIN + 1)
    chosen = jax.random.randint(spot_key, (), 0, FRAMES)
    return jnp.where(jnp.arange(FRAMES) == chosen, WIN, drawn).astype(jnp.int32)


def set_ends(values, key, smallest, largest):
    longest = values.shape.index(max(values.shape))
    spots = []
    for shift in (0, 1):
        where = [jax.random.randint(jax.random.fold_in(key, axis), (), 0, length) for axis, length in enumerate(values.shape)]
        where[longest] = (where[longest] + shift) % values.shape[longest]
        spots.append(tuple(where))
    return values.at[spots[0]].set(smallest).at[spots[1]].set(largest)


def steps_of(key, extent, shards, smallest, largest):
    loudness = 1.0
    for axis_at, shards_of in shards:
        draws = jax.random.uniform(jax.random.fold_in(jax.random.fold_in(key, 6), axis_at), (shards_of,), jnp.float32, smallest / len(shards), largest / len(shards))
        loudness = loudness * jnp.repeat(jnp.exp(draws), extent[axis_at] // shards_of).reshape((-1,) + (1,) * (len(extent) - 1 - axis_at))
    return loudness


def scatter_about(key, dims, deviation, limit, shards=(), held_as=jnp.bfloat16):
    gain = steps_of(key, dims, shards, -0.22, 0.18) if shards else 1.0
    values = jax.random.normal(key, dims, jnp.float32) * deviation * gain
    return jnp.minimum(jnp.maximum(values, -limit), limit).astype(held_as)


def setup_inputs(seed: int = 0, part: int = 0) -> dict:
    splits = jax.random.split(jax.random.key(seed), 14)
    own_keys = jax.random.split(jax.random.fold_in(splits[13], part), 14)
    return {
        "clean_keys": draw_clean_keys(jax.random.fold_in(jax.random.fold_in(splits[13], part), 71), part),
        "clean_values": draw_clean_values(jax.random.fold_in(jax.random.fold_in(splits[13], part), 71), part),
        "clean_rates": draw_clean_rates(jax.random.fold_in(jax.random.fold_in(splits[13], part), 71), part),
        "w_in": scatter_about(splits[3], (H, DH, DH), DH ** -0.5, 0.25),
        "w_gate": scatter_about(splits[4], (H, DH, DH), DH ** -0.5, 0.25),
        "w_out": scatter_about(splits[5], (H, DH, DH), DH ** -0.5, 0.25),
        "noisy_tokens": draw_noisy_tokens(jax.random.fold_in(jax.random.fold_in(splits[13], part), 71), part),
        "swa_keys": draw_swa_keys(jax.random.fold_in(jax.random.fold_in(splits[13], part), 71), part),
        "swa_values": scatter_about(own_keys[8], (TOKENS, D), 5.0, 30.0, ((0, 32),)),
        "level_ids": set_ends(jax.random.randint(own_keys[9], (FRAMES,), 0, NLEVEL), jax.random.fold_in(own_keys[9], 1), 0, NLEVEL - 1).astype(jnp.int32),
        "window_reach": draw_window_reach(jax.random.fold_in(jax.random.fold_in(splits[13], part), 71), part),
        "level_mod": scatter_about(splits[11], (NLEVEL, 2 * D), 0.5, 3.0, (), jnp.float32),
        "mem_gain": jnp.clip(1.0 + 0.18 * jax.random.normal(splits[12], (D,), jnp.float32), 0.1, 1.9),
    }


epsilon = 1e-06
update_step = 0.05

def rounded(value):
    return lax.optimization_barrier(value.astype(jnp.bfloat16)).astype(jnp.float32)

def gradient_block(key_rows, value_rows, rate_rows, w_in, w_gate, w_out):
    row_count = key_rows.shape[0]
    key_heads = key_rows.reshape(row_count, H, DH).astype(jnp.float32)
    value_heads = value_rows.reshape(row_count, H, DH).astype(jnp.float32)
    first_proj = jnp.einsum('thd,hfd->thf', key_heads, w_in.astype(jnp.float32))
    second = jnp.einsum('thd,hfd->thf', key_heads, w_gate.astype(jnp.float32))
    sigmoid = jax.nn.sigmoid(first_proj)
    active = first_proj * sigmoid
    hidden = rounded(active * second)
    scaled = rounded(rate_rows[:, :, None] * value_heads)
    d_act = jnp.einsum('thd,hdf->thf', scaled, w_out.astype(jnp.float32))
    d_first = rounded(d_act * second * sigmoid * (1.0 + first_proj * (1.0 - sigmoid)))
    d_second = rounded(d_act * active)
    g_in = jnp.einsum('thf,thd->hfd', d_first, key_heads)
    g_gate = jnp.einsum('thf,thd->hfd', d_second, key_heads)
    g_out = jnp.einsum('thd,thf->hdf', scaled, hidden)
    return jnp.stack([g_in, g_gate, g_out])

def window_attention(noisy_tokens, swa_keys, swa_values, window_reach):
    head_count = D // SWDH
    query_span = 512 if TOKENS % 512 == 0 else BLOCK
    key_pad = jnp.concatenate([jnp.zeros((WIN, D), swa_keys.dtype), swa_keys], axis=0)
    value_pad = jnp.concatenate([jnp.zeros((WIN, D), swa_values.dtype), swa_values], axis=0)
    reach_all = jnp.repeat(window_reach, BLOCK)

    def attend(block_index):
        row_start = (block_index * query_span).astype(jnp.int32)
        queries = lax.dynamic_slice_in_dim(noisy_tokens, row_start, query_span, 0)
        queries = queries.reshape(query_span, head_count, SWDH).astype(jnp.float32)
        key_block = lax.dynamic_slice_in_dim(key_pad, row_start, query_span + WIN, 0)
        key_block = key_block.reshape(query_span + WIN, head_count, SWDH).astype(jnp.float32)
        value_block = lax.dynamic_slice_in_dim(value_pad, row_start, query_span + WIN, 0)
        value_block = value_block.reshape(query_span + WIN, head_count, SWDH).astype(jnp.float32)
        reach_rows = lax.dynamic_slice_in_dim(reach_all, row_start, query_span, 0)
        query_pos = row_start + jnp.arange(query_span, dtype=jnp.int32)
        key_pos = row_start - WIN + jnp.arange(query_span + WIN, dtype=jnp.int32)
        visible = (key_pos[None, :] <= query_pos[:, None]) & (key_pos[None, :] > query_pos[:, None] - reach_rows[:, None]) & (key_pos[None, :] >= 0)
        scores = jnp.einsum('qsd,ksd->sqk', queries, key_block) * SWDH ** (-0.5)
        scores = jnp.where(visible[None, :, :], scores, -1e+30)
        row_max = lax.optimization_barrier(jnp.max(scores, axis=-1, keepdims=True))
        weights = jnp.exp(scores - row_max)
        totals = lax.optimization_barrier(jnp.sum(weights, axis=-1))
        attended = jnp.einsum('sqk,ksd->qsd', rounded(weights), value_block)
        attended = attended / jnp.transpose(totals)[:, :, None]
        return attended.reshape(query_span, D)
    blocks = lax.map(attend, jnp.arange(TOKENS // query_span, dtype=jnp.int32))
    return blocks.reshape(TOKENS, D)

def reference(clean_keys, clean_values, clean_rates, w_in, w_gate, w_out, noisy_tokens, swa_keys, swa_values, level_ids, window_reach, level_mod, mem_gain):
    grad_span = 2048 if TOKENS % 2048 == 0 else TOKENS

    def accumulate(grad_sum, block_index):
        row_start = (block_index * grad_span).astype(jnp.int32)

        def cut_rows(array):
            return lax.dynamic_slice_in_dim(array, row_start, grad_span, 0)
        return (grad_sum + gradient_block(cut_rows(clean_keys), cut_rows(clean_values), cut_rows(clean_rates), w_in, w_gate, w_out), None)
    grad_sum, unused = lax.scan(accumulate, jnp.zeros((3, H, DH, DH), jnp.float32), jnp.arange(TOKENS // grad_span, dtype=jnp.int32))
    initial = jnp.stack([w_in, w_gate, w_out]).astype(jnp.float32)
    grad_scale = lax.rsqrt(jnp.mean(grad_sum * grad_sum) + epsilon)
    update = initial + update_step * grad_sum * grad_scale
    target = jnp.sqrt(lax.optimization_barrier(jnp.mean(initial * initial, axis=-1, keepdims=True)))
    memories = rounded(update * target * lax.rsqrt(lax.optimization_barrier(jnp.mean(update * update, axis=-1, keepdims=True)) + epsilon))
    noisy_rows = noisy_tokens.astype(jnp.float32)
    inverse = lax.rsqrt(lax.optimization_barrier(jnp.mean(noisy_rows * noisy_rows, axis=-1, keepdims=True)) + epsilon)
    modulation = jnp.repeat(level_mod[level_ids], BLOCK, axis=0)
    queries = rounded(noisy_rows * inverse * (1.0 + modulation[:, :D]) + modulation[:, D:])
    query_heads = queries.reshape(TOKENS, H, DH)
    first_proj = jnp.einsum('thd,hfd->thf', query_heads, memories[0])
    second = jnp.einsum('thd,hfd->thf', query_heads, memories[1])
    mixture = rounded(jax.nn.silu(first_proj) * second)
    recalled = jnp.einsum('thf,hdf->thd', mixture, memories[2])
    recalled = recalled * lax.rsqrt(lax.optimization_barrier(jnp.mean(recalled * recalled, axis=-1, keepdims=True)) + epsilon) * mem_gain.reshape(H, DH)
    attended = window_attention(noisy_tokens, swa_keys, swa_values, window_reach)
    return (recalled.reshape(TOKENS, D) + attended).astype(jnp.bfloat16)
```

```python
import functools

import jax
import jax.numpy as jnp
from jax import lax
from jax.experimental import pallas as pl
from jax.experimental.pallas import tpu as pltpu
from jax.sharding import PartitionSpec as P

SWDH = 128
WIN = 1024
BLOCK = 128

epsilon = 1e-06
update_step = 0.05


def attend_kernel(reach_ref, first_ref, q_ref, kp_ref, kc_ref, vp_ref, vc_ref, o_ref, k_all, v_all):
    b = pl.program_id(1)
    prev = kp_ref.shape[0]
    span = WIN + BLOCK

    @pl.when(b == 0)
    def _():
        k_all[:prev] = kp_ref[...]
        k_all[prev:] = kc_ref[...]
        v_all[:prev] = vp_ref[...]
        v_all[prev:] = vc_ref[...]

    start = pl.multiple_of(prev - WIN + b * BLOCK, BLOCK)
    keys = k_all[pl.ds(start, span), :]
    values = v_all[pl.ds(start, span), :]
    scores = lax.dot_general(
        q_ref[...], keys, (((1,), (1,)), ((), ())), preferred_element_type=jnp.float32
    ) * SWDH ** (-0.5)
    row = lax.broadcasted_iota(jnp.int32, (BLOCK, span), 0)
    col = lax.broadcasted_iota(jnp.int32, (BLOCK, span), 1)
    ahead = col - row
    oldest = -first_ref[0] - b * BLOCK + WIN
    visible = (ahead <= WIN) & (ahead > WIN - reach_ref[b]) & (col >= oldest)
    scores = jnp.where(visible, scores, -1e30)
    weights = jnp.exp(scores - jnp.max(scores, axis=-1, keepdims=True))
    totals = jnp.sum(weights, axis=-1, keepdims=True)
    o_ref[...] = (
        jnp.dot(weights.astype(jnp.bfloat16), values, preferred_element_type=jnp.float32) / totals
    )


def attend(reach, first, z, k_prev, k, v_prev, v, head_start, heads):
    rows = z.shape[0]
    prev = k_prev.shape[0]
    blocks = rows // BLOCK
    whole = lambda n: pl.BlockSpec((n, SWDH), lambda h, b, *_: (0, head_start + h))
    return pl.pallas_call(
        attend_kernel,
        out_shape=jax.ShapeDtypeStruct((rows, heads * SWDH), jnp.float32),
        grid_spec=pltpu.PrefetchScalarGridSpec(
            num_scalar_prefetch=2,
            grid=(heads, blocks),
            in_specs=[
                pl.BlockSpec((BLOCK, SWDH), lambda h, b, *_: (b, head_start + h)),
                whole(prev),
                whole(rows),
                whole(prev),
                whole(rows),
            ],
            out_specs=pl.BlockSpec((BLOCK, SWDH), lambda h, b, *_: (b, h)),
            scratch_shapes=[
                pltpu.VMEM((prev + rows, SWDH), jnp.bfloat16),
                pltpu.VMEM((prev + rows, SWDH), jnp.bfloat16),
            ],
        ),
        compiler_params=pltpu.CompilerParams(vmem_limit_bytes=24 * 1024 * 1024),
        cost_estimate=pl.CostEstimate(
            flops=heads * rows * (WIN + BLOCK) * SWDH * 16,
            bytes_accessed=heads * SWDH * (prev + rows) * 8,
            transcendentals=heads * rows * (WIN + BLOCK),
        ),
    )(reach, first, z, k_prev, k, v_prev, v)


def local(
    clean_keys,
    clean_values,
    clean_rates,
    w_in,
    w_gate,
    w_out,
    noisy_tokens,
    swa_keys,
    swa_values,
    level_ids,
    window_reach,
    level_mod,
    mem_gain,
):
    count = clean_keys.shape[0]
    heads, size = w_in.shape[0], w_in.shape[1]
    flat = heads * size
    frames = level_ids.shape[0]
    devices = lax.axis_size("tok")
    position = lax.axis_index("tok")
    mine = position % heads
    group = position // heads
    rows = heads * count
    bf16, f32 = jnp.bfloat16, jnp.float32
    peers = [[g * heads + h for g in range(devices // heads)] for h in range(heads)]

    def swap(block, s):
        return lax.ppermute(block, "tok", [(i, i ^ s) for i in range(devices)])

    def columns(array, head):
        return lax.dynamic_slice_in_dim(array, head * size, size, 1)

    rates = jnp.repeat(clean_rates, size, axis=1)
    scaled_rows = (rates * clean_values.astype(f32)).astype(bf16)
    clean = []
    for s in range(heads):
        piece = jnp.stack([columns(clean_keys, mine ^ s), columns(scaled_rows, mine ^ s)])
        clean.append(piece if s == 0 else swap(piece, s))
    keys = jnp.concatenate([p[0] for p in clean], axis=0)
    scaled = jnp.concatenate([p[1] for p in clean], axis=0)

    square = jnp.mean(jnp.square(noisy_tokens.astype(f32)), axis=-1)
    own = jnp.concatenate([square, level_ids.astype(f32), window_reach.astype(f32)])[None, :]
    facts = jnp.zeros((heads, own.shape[1]), f32)
    for s in range(heads):
        piece = own if s == 0 else swap(own, s)
        facts = lax.dynamic_update_slice(facts, piece, (mine ^ s, 0))

    noisy = jnp.zeros((3, rows, size), bf16)
    for s in range(heads):
        piece = jnp.stack([columns(a, mine ^ s) for a in (noisy_tokens, swa_keys, swa_values)])
        piece = piece if s == 0 else swap(piece, s)
        noisy = lax.dynamic_update_slice(noisy, piece, (0, (mine ^ s) * count, 0))
    z = noisy[0]
    kv = noisy[1:]
    earlier = []
    carried = kv
    for hop in range(-(-WIN // rows)):
        carried = lax.ppermute(
            carried, "tok", [(i, i + heads) for i in range(devices - heads)]
        )
        earlier.insert(0, carried)
    before = earlier[0] if len(earlier) == 1 else jnp.concatenate(earlier, axis=1)

    base = [lax.dynamic_index_in_dim(w, mine, 0, keepdims=False) for w in (w_in, w_gate, w_out)]
    dot = functools.partial(lax.dot_general, preferred_element_type=f32)
    nt, nn, tn = (((1,), (1,)), ((), ())), (((1,), (0,)), ((), ())), (((0,), (0,)), ((), ()))
    first = dot(keys, base[0], nt)
    second = dot(keys, base[1], nt)
    sigmoid = jax.nn.sigmoid(first)
    active = first * sigmoid
    hidden = (active * second).astype(bf16)
    d_act = dot(scaled, base[2], nn)
    d_first = (d_act * second * sigmoid * (1.0 + first * (1.0 - sigmoid))).astype(bf16)
    d_second = (d_act * active).astype(bf16)
    grads = jnp.concatenate(
        [dot(d_first, keys, tn), dot(d_second, keys, tn), dot(scaled, hidden, tn)], axis=0
    )
    share = lax.psum_scatter(
        grads, "tok", scatter_dimension=0, tiled=True, axis_index_groups=peers
    )
    grad = lax.all_gather(
        share.astype(bf16), "tok", axis=0, tiled=True, axis_index_groups=peers
    ).astype(f32)
    own_power = jnp.broadcast_to(jnp.sum(grad * grad), (8, 128))
    power = own_power
    for s in range(1, heads):
        power = power + swap(own_power, s)

    reach = facts[:, count + frames :].reshape(-1).astype(jnp.int32)
    first_token = (group * rows).astype(jnp.int32).reshape(1)
    half = size // SWDH // 2
    attended = jnp.concatenate(
        [
            attend(reach, first_token, z, before[0], kv[0], before[1], kv[1], start, half)
            for start in (0, half)
        ],
        axis=1,
    )

    grad_scale = lax.rsqrt(power[0, 0] / (3 * flat * size) + epsilon)
    initial = jnp.concatenate(base, axis=0).astype(f32)
    update = initial + update_step * grad * grad_scale
    target = jnp.sqrt(jnp.mean(initial * initial, axis=-1, keepdims=True))
    memory = (
        update * target * lax.rsqrt(jnp.mean(update * update, axis=-1, keepdims=True) + epsilon)
    ).astype(bf16)

    inverse = lax.rsqrt(facts[:, :count].reshape(rows, 1) + epsilon)
    levels = facts[:, count : count + frames].reshape(-1).astype(jnp.int32)
    scale = jnp.take(columns(level_mod[:, :flat], mine), levels, axis=0)
    shift = jnp.take(columns(level_mod[:, flat:], mine), levels, axis=0)
    queries = (
        (z.astype(f32) * inverse).reshape(-1, BLOCK, size) * (1.0 + scale[:, None, :])
        + shift[:, None, :]
    ).astype(bf16).reshape(rows, size)
    mixture = (
        jax.nn.silu(dot(queries, memory[:size], nt)) * dot(queries, memory[size : 2 * size], nt)
    ).astype(bf16)
    recalled = dot(mixture, memory[2 * size :], nt)
    gain = lax.dynamic_slice_in_dim(mem_gain, mine * size, size, 0)
    recalled = (
        recalled * lax.rsqrt(jnp.mean(recalled * recalled, axis=-1, keepdims=True) + epsilon) * gain
    )
    done = (recalled + attended).astype(bf16)
    result = jnp.zeros((count, flat), bf16)
    for s in range(heads):
        piece = lax.dynamic_slice_in_dim(done, (mine ^ s) * count, count, 0)
        piece = piece if s == 0 else swap(piece, s)
        result = lax.dynamic_update_slice(result, piece, (0, (mine ^ s) * size))
    return result


def solution(mesh):
    rows = P(("groups", "tok"), None)
    blocks = P(("groups", "tok"))
    return jax.shard_map(
        local,
        mesh=mesh,
        in_specs=(rows, rows, rows, P(), P(), P(), rows, rows, rows, blocks, blocks, P(), P()),
        out_specs=rows,
        check_vma=False,
    )
```

```python
import functools

import jax
import jax.numpy as jnp
from jax import lax
from jax.experimental import pallas as pl
from jax.experimental.pallas import tpu as pltpu
from jax.sharding import PartitionSpec as P

SWDH = 128
WIN = 1024
BLOCK = 128

epsilon = 1e-06
update_step = 0.05


def attend_kernel(reach_ref, first_ref, q_ref, kp_ref, kc_ref, vp_ref, vc_ref, o_ref, k_all, v_all):
    b = pl.program_id(1)
    prev = kp_ref.shape[0]
    span = WIN + BLOCK

    @pl.when(b == 0)
    def _():
        k_all[:prev] = kp_ref[...]
        k_all[prev:] = kc_ref[...]
        v_all[:prev] = vp_ref[...]
        v_all[prev:] = vc_ref[...]

    start = pl.multiple_of(prev - WIN + b * BLOCK, BLOCK)
    keys = k_all[pl.ds(start, span), :]
    values = v_all[pl.ds(start, span), :]
    scores = lax.dot_general(
        q_ref[...], keys, (((1,), (1,)), ((), ())), preferred_element_type=jnp.float32
    ) * SWDH ** (-0.5)
    row = lax.broadcasted_iota(jnp.int32, (BLOCK, span), 0)
    col = lax.broadcasted_iota(jnp.int32, (BLOCK, span), 1)
    ahead = col - row
    oldest = -first_ref[0] - b * BLOCK + WIN
    visible = (ahead <= WIN) & (ahead > WIN - reach_ref[b]) & (col >= oldest)
    scores = jnp.where(visible, scores, -1e30)
    weights = jnp.exp(scores - jnp.max(scores, axis=-1, keepdims=True))
    totals = jnp.sum(weights, axis=-1, keepdims=True)
    o_ref[...] = (
        jnp.dot(weights.astype(jnp.bfloat16), values, preferred_element_type=jnp.float32) / totals
    )


def attend(reach, first, z, k_prev, k, v_prev, v, head_start, heads):
    rows = z.shape[0]
    prev = k_prev.shape[0]
    blocks = rows // BLOCK
    whole = lambda n: pl.BlockSpec((n, SWDH), lambda h, b, *_: (0, head_start + h))
    return pl.pallas_call(
        attend_kernel,
        out_shape=jax.ShapeDtypeStruct((rows, heads * SWDH), jnp.float32),
        grid_spec=pltpu.PrefetchScalarGridSpec(
            num_scalar_prefetch=2,
            grid=(heads, blocks),
            in_specs=[
                pl.BlockSpec((BLOCK, SWDH), lambda h, b, *_: (b, head_start + h)),
                whole(prev),
                whole(rows),
                whole(prev),
                whole(rows),
            ],
            out_specs=pl.BlockSpec((BLOCK, SWDH), lambda h, b, *_: (b, h)),
            scratch_shapes=[
                pltpu.VMEM((prev + rows, SWDH), jnp.bfloat16),
                pltpu.VMEM((prev + rows, SWDH), jnp.bfloat16),
            ],
        ),
        compiler_params=pltpu.CompilerParams(vmem_limit_bytes=24 * 1024 * 1024),
        cost_estimate=pl.CostEstimate(
            flops=heads * rows * (WIN + BLOCK) * SWDH * 16,
            bytes_accessed=heads * SWDH * (prev + rows) * 8,
            transcendentals=heads * rows * (WIN + BLOCK),
        ),
    )(reach, first, z, k_prev, k, v_prev, v)


def local(
    clean_keys,
    clean_values,
    clean_rates,
    w_in,
    w_gate,
    w_out,
    noisy_tokens,
    swa_keys,
    swa_values,
    level_ids,
    window_reach,
    level_mod,
    mem_gain,
):
    count = clean_keys.shape[0]
    heads, size = w_in.shape[0], w_in.shape[1]
    flat = heads * size
    frames = level_ids.shape[0]
    devices = lax.axis_size("tok")
    position = lax.axis_index("tok")
    mine = position % heads
    group = position // heads
    rows = heads * count
    bf16, f32 = jnp.bfloat16, jnp.float32
    assert heads == 4 and devices % 8 == 0

    def crossed(i):
        return (i & ~6) | ((i & 2) << 1) | ((i & 4) >> 1)

    every = range(devices)
    peers = [[i for i in every if i % heads == h] for h in range(heads)]
    clean_peers = [[i for i in every if crossed(i) % heads == h] for h in range(heads)]
    clean_mine = (position & 1) | ((position >> 1) & 2)

    def swap(block, s):
        return lax.ppermute(block, "tok", [(i, i ^ s) for i in every])

    def columns(array, head):
        return lax.dynamic_slice_in_dim(array, head * size, size, 1)

    rates = jnp.repeat(clean_rates, size, axis=1)
    scaled_rows = (rates * clean_values.astype(f32)).astype(bf16)
    clean = []
    for s in range(heads):
        other = clean_mine ^ s
        piece = jnp.stack([columns(clean_keys, other), columns(scaled_rows, other)])
        clean.append(piece if s == 0 else swap(piece, crossed(s)))
    keys = jnp.concatenate([p[0] for p in clean], axis=0)
    scaled = jnp.concatenate([p[1] for p in clean], axis=0)

    square = jnp.mean(jnp.square(noisy_tokens.astype(f32)), axis=-1)
    own = jnp.concatenate([square, level_ids.astype(f32), window_reach.astype(f32)])[None, :]
    facts = jnp.zeros((heads, own.shape[1]), f32)
    for s in range(heads):
        piece = own if s == 0 else swap(own, s)
        facts = lax.dynamic_update_slice(facts, piece, (mine ^ s, 0))

    pieces = []
    for s in range(heads):
        piece = jnp.stack([columns(a, mine ^ s) for a in (noisy_tokens, swa_keys, swa_values)])
        pieces.append(piece if s == 0 else swap(piece, s))
    keys, scaled, pieces[1], pieces[2] = lax.optimization_barrier(
        (keys, scaled, pieces[1], pieces[2])
    )

    def pick(h):
        return [lax.dynamic_index_in_dim(w, h, 0, keepdims=False) for w in (w_in, w_gate, w_out)]

    base = pick(clean_mine)
    dot = functools.partial(lax.dot_general, preferred_element_type=f32)
    nt, nn, tn = (((1,), (1,)), ((), ())), (((1,), (0,)), ((), ())), (((0,), (0,)), ((), ()))
    first = dot(keys, base[0], nt)
    second = dot(keys, base[1], nt)
    sigmoid = jax.nn.sigmoid(first)
    active = first * sigmoid
    hidden = (active * second).astype(bf16)
    d_act = dot(scaled, base[2], nn)
    d_first = (d_act * second * sigmoid * (1.0 + first * (1.0 - sigmoid))).astype(bf16)
    d_second = (d_act * active).astype(bf16)
    d_first, d_second, hidden, pieces[3] = lax.optimization_barrier(
        (d_first, d_second, hidden, pieces[3])
    )
    grads = jnp.concatenate(
        [dot(d_first, keys, tn), dot(d_second, keys, tn), dot(scaled, hidden, tn)], axis=0
    )
    share = lax.psum_scatter(
        grads, "tok", scatter_dimension=0, tiled=True, axis_index_groups=clean_peers
    )
    share = lax.ppermute(share.astype(bf16), "tok", [(i, crossed(i)) for i in every])
    grad = lax.all_gather(
        share, "tok", axis=0, tiled=True, axis_index_groups=peers
    )

    noisy = jnp.zeros((3, rows, size), bf16)
    for s in range(heads):
        noisy = lax.dynamic_update_slice(noisy, pieces[s], (0, (mine ^ s) * count, 0))
    z = noisy[0]
    kv = noisy[1:]
    earlier = []
    carried = kv
    for hop in range(-(-WIN // rows)):
        carried = lax.ppermute(
            carried, "tok", [(i, i + heads) for i in range(devices - heads)]
        )
        earlier.insert(0, carried)
    before = earlier[0] if len(earlier) == 1 else jnp.concatenate(earlier, axis=1)

    reach = facts[:, count + frames :].reshape(-1).astype(jnp.int32)
    first_token = (group * rows).astype(jnp.int32).reshape(1)
    half = size // SWDH // 2
    attended = jnp.concatenate(
        [
            attend(reach, first_token, z, before[0], kv[0], before[1], kv[1], start, half)
            for start in (0, half)
        ],
        axis=1,
    )
    grad, attended = lax.optimization_barrier((grad, attended))
    grad = grad.astype(f32)
    own_power = jnp.broadcast_to(jnp.sum(grad * grad), (8, 128))
    power = own_power
    for s in range(1, heads):
        power = power + swap(own_power, s)

    grad_scale = lax.rsqrt(power[0, 0] / (3 * flat * size) + epsilon)
    initial = jnp.concatenate(pick(mine), axis=0).astype(f32)
    update = initial + update_step * grad * grad_scale
    target = jnp.sqrt(jnp.mean(initial * initial, axis=-1, keepdims=True))
    memory = (
        update * target * lax.rsqrt(jnp.mean(update * update, axis=-1, keepdims=True) + epsilon)
    ).astype(bf16)

    inverse = lax.rsqrt(facts[:, :count].reshape(rows, 1) + epsilon)
    levels = facts[:, count : count + frames].reshape(-1).astype(jnp.int32)
    scale = jnp.take(columns(level_mod[:, :flat], mine), levels, axis=0)
    shift = jnp.take(columns(level_mod[:, flat:], mine), levels, axis=0)
    queries = (
        (z.astype(f32) * inverse).reshape(-1, BLOCK, size) * (1.0 + scale[:, None, :])
        + shift[:, None, :]
    ).astype(bf16).reshape(rows, size)
    mixture = (
        jax.nn.silu(dot(queries, memory[:size], nt)) * dot(queries, memory[size : 2 * size], nt)
    ).astype(bf16)
    recalled = dot(mixture, memory[2 * size :], nt)
    gain = lax.dynamic_slice_in_dim(mem_gain, mine * size, size, 0)
    recalled = (
        recalled * lax.rsqrt(jnp.mean(recalled * recalled, axis=-1, keepdims=True) + epsilon) * gain
    )
    done = (recalled + attended).astype(bf16)
    result = jnp.zeros((count, flat), bf16)
    for s in range(heads):
        piece = lax.dynamic_slice_in_dim(done, (mine ^ s) * count, count, 0)
        piece = piece if s == 0 else swap(piece, s)
        result = lax.dynamic_update_slice(result, piece, (0, (mine ^ s) * size))
    return result


def solution(mesh):
    rows = P(("groups", "tok"), None)
    blocks = P(("groups", "tok"))
    return jax.shard_map(
        local,
        mesh=mesh,
        in_specs=(rows, rows, rows, P(), P(), P(), rows, rows, rows, blocks, blocks, P(), P()),
        out_specs=rows,
        check_vma=False,
    )
```

```python
import functools

import jax
import jax.numpy as jnp
from jax import lax
from jax.experimental import pallas as pl
from jax.experimental.pallas import tpu as pltpu
from jax.sharding import PartitionSpec as P

SWDH = 128
WIN = 1024
BLOCK = 128

epsilon = 1e-06
update_step = 0.05


def attend_kernel(reach_ref, first_ref, q_ref, kp_ref, kc_ref, vp_ref, vc_ref, o_ref, k_all, v_all):
    b = pl.program_id(1)
    prev = kp_ref.shape[0]
    span = WIN + BLOCK

    @pl.when(b == 0)
    def _():
        k_all[:prev] = kp_ref[...]
        k_all[prev:] = kc_ref[...]
        v_all[:prev] = vp_ref[...]
        v_all[prev:] = vc_ref[...]

    start = pl.multiple_of(prev - WIN + b * BLOCK, BLOCK)
    keys = k_all[pl.ds(start, span), :]
    values = v_all[pl.ds(start, span), :]
    scores = lax.dot_general(
        q_ref[...], keys, (((1,), (1,)), ((), ())), preferred_element_type=jnp.float32
    ) * SWDH ** (-0.5)
    row = lax.broadcasted_iota(jnp.int32, (BLOCK, span), 0)
    col = lax.broadcasted_iota(jnp.int32, (BLOCK, span), 1)
    ahead = col - row
    oldest = -first_ref[0] - b * BLOCK + WIN
    visible = (ahead <= WIN) & (ahead > WIN - reach_ref[b]) & (col >= oldest)
    scores = jnp.where(visible, scores, -1e30)
    weights = jnp.exp(scores - jnp.max(scores, axis=-1, keepdims=True))
    totals = jnp.sum(weights, axis=-1, keepdims=True)
    o_ref[...] = (
        jnp.dot(weights.astype(jnp.bfloat16), values, preferred_element_type=jnp.float32) / totals
    )


def attend(reach, first, z, k_prev, k, v_prev, v, head_start, heads):
    rows = z.shape[0]
    prev = k_prev.shape[0]
    blocks = rows // BLOCK
    whole = lambda n: pl.BlockSpec((n, SWDH), lambda h, b, *_: (0, head_start + h))
    return pl.pallas_call(
        attend_kernel,
        out_shape=jax.ShapeDtypeStruct((rows, heads * SWDH), jnp.float32),
        grid_spec=pltpu.PrefetchScalarGridSpec(
            num_scalar_prefetch=2,
            grid=(heads, blocks),
            in_specs=[
                pl.BlockSpec((BLOCK, SWDH), lambda h, b, *_: (b, head_start + h)),
                whole(prev),
                whole(rows),
                whole(prev),
                whole(rows),
            ],
            out_specs=pl.BlockSpec((BLOCK, SWDH), lambda h, b, *_: (b, h)),
            scratch_shapes=[
                pltpu.VMEM((prev + rows, SWDH), jnp.bfloat16),
                pltpu.VMEM((prev + rows, SWDH), jnp.bfloat16),
            ],
        ),
        compiler_params=pltpu.CompilerParams(vmem_limit_bytes=24 * 1024 * 1024),
        cost_estimate=pl.CostEstimate(
            flops=heads * rows * (WIN + BLOCK) * SWDH * 16,
            bytes_accessed=heads * SWDH * (prev + rows) * 8,
            transcendentals=heads * rows * (WIN + BLOCK),
        ),
    )(reach, first, z, k_prev, k, v_prev, v)


def local(
    clean_keys,
    clean_values,
    clean_rates,
    w_in,
    w_gate,
    w_out,
    noisy_tokens,
    swa_keys,
    swa_values,
    level_ids,
    window_reach,
    level_mod,
    mem_gain,
):
    count = clean_keys.shape[0]
    heads, size = w_in.shape[0], w_in.shape[1]
    flat = heads * size
    frames = level_ids.shape[0]
    devices = lax.axis_size("tok")
    position = lax.axis_index("tok")
    mine = position % heads
    group = position // heads
    rows = heads * count
    bf16, f32 = jnp.bfloat16, jnp.float32
    assert heads == 4 and devices % 8 == 0

    def crossed(i):
        return (i & ~6) | ((i & 2) << 1) | ((i & 4) >> 1)

    every = range(devices)
    peers = [[i for i in every if i % heads == h] for h in range(heads)]
    clean_peers = [[i for i in every if crossed(i) % heads == h] for h in range(heads)]
    clean_mine = (position & 1) | ((position >> 1) & 2)

    def swap(block, s):
        return lax.ppermute(block, "tok", [(i, i ^ s) for i in every])

    def columns(array, head):
        return lax.dynamic_slice_in_dim(array, head * size, size, 1)

    rates = jnp.repeat(clean_rates, size, axis=1)
    scaled_rows = (rates * clean_values.astype(f32)).astype(bf16)
    clean = []
    for s in range(heads):
        other = clean_mine ^ s
        piece = jnp.stack([columns(clean_keys, other), columns(scaled_rows, other)])
        clean.append(piece if s == 0 else swap(piece, crossed(s)))
    keys = jnp.concatenate([p[0] for p in clean], axis=0)
    scaled = jnp.concatenate([p[1] for p in clean], axis=0)

    square = jnp.mean(jnp.square(noisy_tokens.astype(f32)), axis=-1)
    own = jnp.concatenate([square, level_ids.astype(f32), window_reach.astype(f32)])[None, :]
    facts = jnp.zeros((heads, own.shape[1]), f32)
    for s in range(heads):
        piece = own if s == 0 else swap(own, s)
        facts = lax.dynamic_update_slice(facts, piece, (mine ^ s, 0))

    pieces = []
    for s in range(heads):
        piece = jnp.stack([columns(a, mine ^ s) for a in (noisy_tokens, swa_keys, swa_values)])
        pieces.append(piece if s == 0 else swap(piece, s))
    keys, scaled, pieces[1], pieces[2] = lax.optimization_barrier(
        (keys, scaled, pieces[1], pieces[2])
    )

    def pick(h):
        return [lax.dynamic_index_in_dim(w, h, 0, keepdims=False) for w in (w_in, w_gate, w_out)]

    base = pick(clean_mine)
    dot = functools.partial(lax.dot_general, preferred_element_type=f32)
    nt, nn, tn = (((1,), (1,)), ((), ())), (((1,), (0,)), ((), ())), (((0,), (0,)), ((), ()))
    first = dot(keys, base[0], nt)
    second = dot(keys, base[1], nt)
    sigmoid = jax.nn.sigmoid(first)
    active = first * sigmoid
    hidden = (active * second).astype(bf16)
    d_act = dot(scaled, base[2], nn)
    d_first = (d_act * second * sigmoid * (1.0 + first * (1.0 - sigmoid))).astype(bf16)
    d_second = (d_act * active).astype(bf16)
    d_first, d_second, hidden, pieces[3] = lax.optimization_barrier(
        (d_first, d_second, hidden, pieces[3])
    )
    grads = jnp.concatenate(
        [dot(d_first, keys, tn), dot(d_second, keys, tn), dot(scaled, hidden, tn)], axis=0
    )
    fellows = len(clean_peers[0])
    ranks = {i: r for row in clean_peers for r, i in enumerate(row)}
    rank = jnp.array([ranks[i] for i in every], jnp.int32)[position]
    depth = grads.shape[0] // fellows
    share = lax.dynamic_slice_in_dim(grads, rank * depth, depth, 0)
    for s in range(1, fellows):
        route = [(row[r], row[(r + s) % fellows]) for row in clean_peers for r in range(fellows)]
        block = lax.dynamic_slice_in_dim(grads, (rank + s) % fellows * depth, depth, 0)
        share = share + lax.ppermute(block, "tok", route)
    share = lax.ppermute(share.astype(bf16), "tok", [(i, crossed(i)) for i in every])
    grad = lax.all_gather(
        share, "tok", axis=0, tiled=True, axis_index_groups=peers
    )

    noisy = jnp.zeros((3, rows, size), bf16)
    for s in range(heads):
        noisy = lax.dynamic_update_slice(noisy, pieces[s], (0, (mine ^ s) * count, 0))
    z = noisy[0]
    kv = noisy[1:]
    earlier = []
    carried = kv
    for hop in range(-(-WIN // rows)):
        carried = lax.ppermute(
            carried, "tok", [(i, i + heads) for i in range(devices - heads)]
        )
        earlier.insert(0, carried)
    before = earlier[0] if len(earlier) == 1 else jnp.concatenate(earlier, axis=1)

    reach = facts[:, count + frames :].reshape(-1).astype(jnp.int32)
    first_token = (group * rows).astype(jnp.int32).reshape(1)
    half = size // SWDH // 2
    attended = jnp.concatenate(
        [
            attend(reach, first_token, z, before[0], kv[0], before[1], kv[1], start, half)
            for start in (0, half)
        ],
        axis=1,
    )
    grad, attended = lax.optimization_barrier((grad, attended))
    grad = grad.astype(f32)
    own_power = jnp.broadcast_to(jnp.sum(grad * grad), (8, 128))
    power = own_power
    for s in range(1, heads):
        power = power + swap(own_power, s)

    grad_scale = lax.rsqrt(power[0, 0] / (3 * flat * size) + epsilon)
    initial = jnp.concatenate(pick(mine), axis=0).astype(f32)
    update = initial + update_step * grad * grad_scale
    target = jnp.sqrt(jnp.mean(initial * initial, axis=-1, keepdims=True))
    memory = (
        update * target * lax.rsqrt(jnp.mean(update * update, axis=-1, keepdims=True) + epsilon)
    ).astype(bf16)

    inverse = lax.rsqrt(facts[:, :count].reshape(rows, 1) + epsilon)
    levels = facts[:, count : count + frames].reshape(-1).astype(jnp.int32)
    scale = jnp.take(columns(level_mod[:, :flat], mine), levels, axis=0)
    shift = jnp.take(columns(level_mod[:, flat:], mine), levels, axis=0)
    queries = (
        (z.astype(f32) * inverse).reshape(-1, BLOCK, size) * (1.0 + scale[:, None, :])
        + shift[:, None, :]
    ).astype(bf16).reshape(rows, size)
    mixture = (
        jax.nn.silu(dot(queries, memory[:size], nt)) * dot(queries, memory[size : 2 * size], nt)
    ).astype(bf16)
    recalled = dot(mixture, memory[2 * size :], nt)
    gain = lax.dynamic_slice_in_dim(mem_gain, mine * size, size, 0)
    recalled = (
        recalled * lax.rsqrt(jnp.mean(recalled * recalled, axis=-1, keepdims=True) + epsilon) * gain
    )
    done = (recalled + attended).astype(bf16)
    result = jnp.zeros((count, flat), bf16)
    for s in range(heads):
        piece = lax.dynamic_slice_in_dim(done, (mine ^ s) * count, count, 0)
        piece = piece if s == 0 else swap(piece, s)
        result = lax.dynamic_update_slice(result, piece, (0, (mine ^ s) * size))
    return result


def solution(mesh):
    rows = P(("groups", "tok"), None)
    blocks = P(("groups", "tok"))
    return jax.shard_map(
        local,
        mesh=mesh,
        in_specs=(rows, rows, rows, P(), P(), P(), rows, rows, rows, blocks, blocks, P(), P()),
        out_specs=rows,
        check_vma=False,
    )
```
